256 devices in a mesh: inp: 4 (over x), wt: 4 (over y_lo, core), dep: 16 (over z, y_hi).
Axes of the slice: x: 4, y: 4 (y_hi: 2, y_lo: 2; y = y_hi * 2 + y_lo), z: 8, core: 2. Of those that a mesh axis runs over, the one named last changes fastest.
Arguments:
- tokens: bfloat16 [1024, 8192], P(('wt', 'inp'), 'dep'), may hold values from -6 to 6
- w_gate: bfloat16 [8192, 14336], P('dep', ('inp', 'wt')), may hold values from -0.0625 to 0.0625
- w_up: bfloat16 [8192, 14336], P('dep', ('inp', 'wt')), may hold values from -0.0625 to 0.0625
- w_down: bfloat16 [14336, 8192], P(('inp', 'wt'), 'dep'), may hold values from -0.046875 to 0.046875
- grad_out: bfloat16 [1024, 8192], P(('wt', 'inp'), 'dep'), may hold values from -6 to 6
Outputs:
- mixed: bfloat16 [1024, 8192], P(('wt', 'inp'), 'dep')
- grad_tokens: bfloat16 [1024, 8192], P(('wt', 'inp'), 'dep')
- grad_w_gate: bfloat16 [8192, 14336], P('dep', ('inp', 'wt'))
- grad_w_up: bfloat16 [8192, 14336], P('dep', ('inp', 'wt'))
- grad_w_down: bfloat16 [14336, 8192], P(('inp', 'wt'), 'dep')
The draws below stay inside these ranges and needn't reach their ends.
All inputs are finite; a program needn't handle non-finite values.
Results may differ from the reference program's by a relative error of at most 0.035.
Values may be sent and summed in bfloat16 or wider, within the bound.
No kernel may reach another device: no remote copies, remote signals or barrier semaphores. Data moves between devices by JAX's collectives and lax.ppermute only.
A program may use at most 128 MiB of HBM per device.

```python
import math
import jax
import jax.numpy as jnp
from jax import lax

D = 8192
FF = 14336
TOK_BLK = 256
TOKENS = 1024
N_WT = 4
N_DEP = 16


def level_of(stream_key, dims, cuts, low, largest):
    level = 1.0
    for dim, parts in cuts:
        heights = jax.random.uniform(jax.random.fold_in(jax.random.fold_in(stream_key, 6), dim), (parts,), jnp.float32, low / len(cuts), largest / len(cuts))
        level = level * jnp.repeat(jnp.exp(heights), dims[dim] // parts).reshape((-1,) + (1,) * (len(dims) - 1 - dim))
    return level


def normal_values(own_key, dims, deviation, bound, shards=(), held_as=jnp.bfloat16):
    entries = jax.random.normal(own_key, dims, jnp.float32) * deviation
    if len(shards) > 0:
        entries = level_of(own_key, dims, shards, -0.22, 0.18) * entries
    return jnp.clip(entries, min=-bound, max=bound).astype(held_as)


def setup_inputs(seed: int = 0) -> dict:
    seeds = jax.random.split(jax.random.key(seed), 6)
    return {
        "tokens": normal_values(seeds[0], (TOKENS, D), 1.0, 6.0, ((0, 16), (1, 16))),
        "w_gate": normal_values(seeds[1], (D, FF), D ** -0.5, 0.0625, ((0, 16), (1, 16))),
        "w_up": normal_values(seeds[2], (D, FF), D ** -0.5, 0.0625, ((0, 16), (1, 16))),
        "w_down": normal_values(seeds[3], (FF, D), FF ** -0.5, 0.046875, ((0, 16), (1, 16))),
        "grad_out": normal_values(seeds[4], (TOKENS, D), 1.0, 6.0, ((0, 16), (1, 16))),
    }


def block_sum(left_blocks, right_blocks, contract, out_shape):

    def add_block(running, block_pair):
        product = lax.dot_general(block_pair[0], block_pair[1], (contract, ((), ())), preferred_element_type=jnp.float32)
        rounded = lax.optimization_barrier(product.astype(jnp.bfloat16)).astype(jnp.float32)
        return (running + rounded, None)
    running, unused = lax.scan(add_block, jnp.zeros(out_shape, jnp.float32), (left_blocks, right_blocks))
    return running

def reference(tokens, w_gate, w_up, w_down, grad_out):
    block_width = D // N_DEP
    token_blocks = tokens.reshape(TOKENS, N_DEP, block_width).transpose(1, 0, 2)
    gate_sum = block_sum(token_blocks, w_gate.reshape(N_DEP, block_width, FF), ((1,), (0,)), (TOKENS, FF))
    up_sum = block_sum(token_blocks, w_up.reshape(N_DEP, block_width, FF), ((1,), (0,)), (TOKENS, FF))
    sigmoid_gate = jax.nn.sigmoid(gate_sum)
    silu_gate = gate_sum * sigmoid_gate
    hidden = (silu_gate * up_sum).astype(jnp.bfloat16)
    mixed = jnp.dot(hidden, w_down, preferred_element_type=jnp.float32).astype(jnp.bfloat16)
    grad_blocks = grad_out.reshape(TOKENS, N_DEP, block_width).transpose(1, 0, 2)
    down_blocks = w_down.reshape(FF, N_DEP, block_width).transpose(1, 0, 2)
    grad_hidden = block_sum(grad_blocks, down_blocks, ((1,), (1,)), (TOKENS, FF))
    grad_gate = (grad_hidden * up_sum * sigmoid_gate * (1.0 + gate_sum * (1.0 - sigmoid_gate))).astype(jnp.bfloat16)
    grad_up = (grad_hidden * silu_gate).astype(jnp.bfloat16)
    back_dims = (((1,), (1,)), ((), ()))
    grad_tokens = (lax.dot_general(grad_gate, w_gate, back_dims, preferred_element_type=jnp.float32) + lax.dot_general(grad_up, w_up, back_dims, preferred_element_type=jnp.float32)).astype(jnp.bfloat16)
    grad_scale = 1.0 / math.sqrt(TOKENS)
    token_rows = tokens.reshape(N_WT, TOK_BLK, D)
    grad_w_gate = (block_sum(token_rows, grad_gate.reshape(N_WT, TOK_BLK, FF), ((0,), (0,)), (D, FF)) * grad_scale).astype(jnp.bfloat16)
    grad_w_up = (block_sum(token_rows, grad_up.reshape(N_WT, TOK_BLK, FF), ((0,), (0,)), (D, FF)) * grad_scale).astype(jnp.bfloat16)
    grad_w_down = (block_sum(hidden.reshape(N_WT, TOK_BLK, FF), grad_out.reshape(N_WT, TOK_BLK, D), ((0,), (0,)), (FF, D)) * grad_scale).astype(jnp.bfloat16)
    return (mixed, grad_tokens, grad_w_gate, grad_w_up, grad_w_down)
```

```python
import math

import jax
import jax.numpy as jnp
from jax import lax
from jax.sharding import Mesh, PartitionSpec as P

BACK_DIMS = (((1,), (1,)), ((), ()))
ROWS_DIMS = (((0,), (0,)), ((), ()))
FINE_AXES = ("x", "yl", "core", "z", "yh")
BF16 = jnp.bfloat16
F32 = jnp.float32


def dot32(left, right, dims=(((1,), (0,)), ((), ()))):
    return lax.dot_general(left, right, dims, preferred_element_type=F32)


def shifted(value, axis, step):
    size = lax.axis_size(axis)
    return lax.ppermute(value, axis, [(i, (i + step) % size) for i in range(size)])


def gather_tokens(block):
    by_x = jnp.concatenate([block] + [shifted(block, "x", -dx) for dx in (1, 2, 3)], axis=0)
    by_y = jnp.concatenate([by_x, shifted(by_x, "yl", 1)], axis=0)
    return jnp.concatenate([by_y, shifted(by_y, "core", 1)], axis=0)


def scatter_tokens(partial):
    rows = partial.shape[0]
    by_core = partial[: rows // 2] + shifted(partial[rows // 2 :], "core", 1)
    by_y = by_core[: rows // 4] + shifted(by_core[rows // 4 :], "yl", 1)
    block = rows // 16
    total = by_y[:block].astype(F32)
    for dx in (1, 2, 3):
        total = total + shifted(by_y[dx * block : (dx + 1) * block], "x", dx).astype(F32)
    return total.astype(BF16)


def block_index(offset, other):
    z = lax.rem(lax.axis_index("z") + offset + 8, 8)
    yh = lax.axis_index("yh")
    return 2 * z + (1 - yh if other else yh)


def block_of(blocks, offset, other):
    return lax.dynamic_index_in_dim(blocks, block_index(offset, other), 0, keepdims=False)


RINGS = ((True, 1, 4), (True, -1, 3), (False, 1, 3), (False, -1, 4))


def reduce_dep(partial):
    blocks = partial.reshape((16, partial.shape[0] // 16, partial.shape[1]))
    sums = [block_of(blocks, way * steps, other) for other, way, steps in RINGS]
    for step in range(4):
        for ring, (other, way, steps) in enumerate(RINGS):
            if step >= steps:
                continue
            came = shifted(sums[ring], "z", way)
            left = steps - 1 - step
            if left > 0:
                source, came = lax.optimization_barrier((blocks, came))
                came = came + block_of(source, way * left, other)
            sums[ring] = came
    theirs = (
        block_of(blocks, 0, True).astype(F32) + sums[0].astype(F32) + sums[1].astype(F32)
    ).astype(BF16)
    came = shifted(theirs, "yh", 1)
    return (
        block_of(blocks, 0, False).astype(F32)
        + sums[2].astype(F32)
        + sums[3].astype(F32)
        + came.astype(F32)
    )


def gather_dep(mine):
    theirs = shifted(mine, "yh", 1)
    whole = jnp.zeros((16,) + mine.shape, mine.dtype)
    for other, value in ((False, mine), (True, theirs)):
        whole = lax.dynamic_update_index_in_dim(whole, value, block_index(0, other), 0)
    held = [theirs if other else mine for other, _, _ in RINGS]
    for step in range(4):
        for ring, (other, way, steps) in enumerate(RINGS):
            if step >= steps:
                continue
            held[ring] = shifted(held[ring], "z", way)
            whole = lax.dynamic_update_index_in_dim(
                whole, held[ring], block_index(-way * (step + 1), other), 0
            )
    return whole.reshape((16 * mine.shape[0], mine.shape[1]))


def body(tokens, w_gate, w_up, w_down, grad_out):
    width = w_gate.shape[1]
    w_both = jnp.concatenate([w_gate, w_up], axis=1)
    all_tokens = gather_tokens(tokens)
    all_grads = gather_tokens(grad_out)
    both = reduce_dep(dot32(all_tokens, w_both).astype(BF16))
    gate_sum, up_sum = both[:, :width], both[:, width:]
    grad_hidden = reduce_dep(dot32(all_grads, w_down, BACK_DIMS).astype(BF16))
    sigmoid_gate = jax.nn.sigmoid(gate_sum)
    hidden = gather_dep((gate_sum * sigmoid_gate * up_sum).astype(BF16))
    gate_part = (
        grad_hidden * up_sum * sigmoid_gate * (1.0 + gate_sum * (1.0 - sigmoid_gate))
    ).astype(BF16)
    up_part = (grad_hidden * (gate_sum * sigmoid_gate)).astype(BF16)
    grad_both = gather_dep(jnp.concatenate([gate_part, up_part], axis=1))
    mixed = scatter_tokens(dot32(hidden, w_down).astype(BF16))
    grad_tokens = scatter_tokens(dot32(grad_both, w_both, BACK_DIMS).astype(BF16))
    grad_scale = 1.0 / math.sqrt(all_tokens.shape[0])
    grad_w_gate = (dot32(all_tokens, grad_both[:, :width], ROWS_DIMS) * grad_scale).astype(BF16)
    grad_w_up = (dot32(all_tokens, grad_both[:, width:], ROWS_DIMS) * grad_scale).astype(BF16)
    grad_w_down = (dot32(hidden, all_grads, ROWS_DIMS) * grad_scale).astype(BF16)
    return (mixed, grad_tokens, grad_w_gate, grad_w_up, grad_w_down)


def solution(mesh):
    fine = Mesh(mesh.devices.reshape((4, 2, 2, 8, 2)), FINE_AXES)
    token_spec = P(("yl", "core", "x"), ("z", "yh"))
    in_specs = (
        token_spec,
        P(("z", "yh"), ("x", "yl", "core")),
        P(("z", "yh"), ("x", "yl", "core")),
        P(("x", "yl", "core"), ("z", "yh")),
        token_spec,
    )
    out_specs = (token_spec, token_spec) + in_specs[1:4]
    return jax.shard_map(body, mesh=fine, in_specs=in_specs, out_specs=out_specs, check_vma=False)
```

```python
import math

import jax
import jax.numpy as jnp
from jax import lax
from jax.sharding import Mesh, PartitionSpec as P

BACK_DIMS = (((1,), (1,)), ((), ()))
ROWS_DIMS = (((0,), (0,)), ((), ()))
FINE_AXES = ("x", "yl", "core", "z", "yh")
PLANE = ("yl", "x")
BF16 = jnp.bfloat16
F32 = jnp.float32
PLUS_FOUR = ((1, 4), (-1, 3))
MINUS_FOUR = ((-1, 4), (1, 3))


def dot32(left, right, dims=(((1,), (0,)), ((), ()))):
    return lax.dot_general(left, right, dims, preferred_element_type=F32)


def shifted(value, axis, step):
    size = lax.axis_size(axis)
    return lax.ppermute(value, axis, [(i, (i + step) % size) for i in range(size)])


def z_at(offset):
    return lax.rem(lax.axis_index("z") + offset + 8, 8)


def pick(blocks, index):
    return lax.dynamic_index_in_dim(blocks, index, 0, keepdims=False)


def put(whole, value, index):
    return lax.dynamic_update_index_in_dim(whole, value, index, 0)


def ordered(axis, mine, theirs):
    first = lax.axis_index(axis) == 0
    return jnp.concatenate(
        [jnp.where(first, mine, theirs), jnp.where(first, theirs, mine)], axis=0
    )


def gather_plane(block, name):
    with jax.named_scope(name + "_plane"):
        copies = jnp.broadcast_to(block[None], (8,) + block.shape)
        plane = lax.all_to_all(copies, PLANE, 0, 0, tiled=True)
        return plane.reshape((8 * block.shape[0], block.shape[1]))


def gather_core(plane, name):
    with jax.named_scope(name + "_core"):
        copies = jnp.broadcast_to(plane[None], (2,) + plane.shape)
        both = lax.all_to_all(copies, "core", 0, 0, tiled=True)
        return both.reshape((2 * plane.shape[0], plane.shape[1]))


def scatter(partials):
    core = lax.axis_index("core")
    halves = [p.reshape((2, p.shape[0] // 2, p.shape[1])) for p in partials]
    with jax.named_scope("outputs_core"):
        sent = jnp.concatenate([pick(h, 1 - core) for h in halves], axis=1)
        total = jnp.concatenate([pick(h, core) for h in halves], axis=1) + shifted(sent, "core", 1)
    with jax.named_scope("outputs_plane"):
        blocks = total.reshape((8, total.shape[0] // 8, total.shape[1]))
        came = lax.all_to_all(blocks, PLANE, 0, 0, tiled=True)
        total = jnp.sum(came.astype(F32), axis=0).astype(BF16)
        width = partials[0].shape[1]
        return total[:, :width], total[:, width:]


class SumRing:
    def __init__(self, name, terms, ways):
        self.name, self.ways = name, ways
        self.blocks = terms.reshape((8, terms.shape[0] // 8, terms.shape[1]))
        self.held = [pick(self.blocks, z_at(way * steps)) for way, steps in ways]

    def step(self, number):
        for ring, (way, steps) in enumerate(self.ways):
            left = steps - number
            if left < 0:
                continue
            with jax.named_scope(self.name):
                came = shifted(self.held[ring], "z", way)
                if left > 0:
                    source, came = lax.optimization_barrier((self.blocks, came))
                    came = came + pick(source, z_at(way * left))
                self.held[ring] = came

    def total(self, ahead=None):
        value = pick(self.blocks, z_at(0)).astype(F32)
        for came in self.held:
            value = value + came.astype(F32)
        yh = lax.axis_index("yh")
        halves = value.reshape((2, value.shape[0] // 2, value.shape[1]))
        with jax.named_scope(self.name + "_yh"):
            sent = pick(halves, 1 - yh).astype(BF16)
            if ahead is not None:
                sent = sent + ahead[:1, :1] * 0
            came = shifted(sent, "yh", 1)
            return pick(halves, yh) + came.astype(F32)


class CopyRing:
    def __init__(self, name, mine, ways):
        self.name, self.ways = name, ways
        with jax.named_scope(name + "_yh"):
            pair = ordered("yh", mine, shifted(mine, "yh", 1))
        self.held = [pair for _ in ways]
        self.whole = put(jnp.zeros((8,) + pair.shape, pair.dtype), pair, z_at(0))

    def step(self, number):
        for ring, (way, steps) in enumerate(self.ways):
            if number <= steps:
                with jax.named_scope(self.name):
                    self.held[ring] = shifted(self.held[ring], "z", way)
                self.whole = put(self.whole, self.held[ring], z_at(-way * number))

    def rows(self):
        return self.whole.reshape((-1, self.whole.shape[2]))


def run(*rings):
    for number in range(1, 5):
        for ring in rings:
            ring.step(number)


def body(tokens, w_gate, w_up, w_down, grad_out):
    tokens = gather_core(gather_plane(tokens, "tokens"), "tokens")
    grads = gather_core(gather_plane(grad_out + tokens[:1, :1] * 0, "grads"), "grads")
    gate = SumRing("gate", dot32(tokens, w_gate).astype(BF16), PLUS_FOUR)
    up = SumRing("up", dot32(tokens, w_up).astype(BF16), MINUS_FOUR)
    down = SumRing("down", dot32(grads, w_down, BACK_DIMS).astype(BF16), PLUS_FOUR)
    run(gate, up, down)
    gate_sum, up_sum = gate.total(), up.total()
    hidden_part = (gate_sum * jax.nn.sigmoid(gate_sum) * up_sum).astype(BF16)
    hidden = CopyRing("hidden", hidden_part, PLUS_FOUR)
    grad_hidden = down.total(hidden_part)
    gate_sum, up_sum = lax.optimization_barrier((gate_sum, up_sum))
    sigmoid_gate = jax.nn.sigmoid(gate_sum)
    grad_gate = CopyRing(
        "grad_gate",
        (
            grad_hidden * up_sum * sigmoid_gate * (1.0 + gate_sum * (1.0 - sigmoid_gate))
        ).astype(BF16),
        MINUS_FOUR,
    )
    grad_up = CopyRing("grad_up", (grad_hidden * (gate_sum * sigmoid_gate)).astype(BF16), PLUS_FOUR)
    run(hidden, grad_gate, grad_up)
    hidden, grad_gate, grad_up = hidden.rows(), grad_gate.rows(), grad_up.rows()
    mixed, grad_tokens = scatter(
        [
            dot32(hidden, w_down).astype(BF16),
            (dot32(grad_gate, w_gate, BACK_DIMS) + dot32(grad_up, w_up, BACK_DIMS)).astype(BF16),
        ]
    )
    grad_scale = 1.0 / math.sqrt(tokens.shape[0])
    with jax.named_scope("weight_grads"):
        grad_w_gate = (dot32(tokens, grad_gate, ROWS_DIMS) * grad_scale).astype(BF16)
        grad_w_up = (dot32(tokens, grad_up, ROWS_DIMS) * grad_scale).astype(BF16)
        grad_w_down = (dot32(hidden, grads, ROWS_DIMS) * grad_scale).astype(BF16)
    return (mixed, grad_tokens, grad_w_gate, grad_w_up, grad_w_down)


def solution(mesh):
    fine = Mesh(mesh.devices.reshape((4, 2, 2, 8, 2)), FINE_AXES)
    token_spec = P(("yl", "core", "x"), ("z", "yh"))
    in_specs = (
        token_spec,
        P(("z", "yh"), ("x", "yl", "core")),
        P(("z", "yh"), ("x", "yl", "core")),
        P(("x", "yl", "core"), ("z", "yh")),
        token_spec,
    )
    out_specs = (token_spec, token_spec) + in_specs[1:4]
    return jax.shard_map(body, mesh=fine, in_specs=in_specs, out_specs=out_specs, check_vma=False)
```

```python
import math

import jax
import jax.numpy as jnp
from jax import lax
from jax.sharding import Mesh, PartitionSpec as P

BACK_DIMS = (((1,), (1,)), ((), ()))
ROWS_DIMS = (((0,), (0,)), ((), ()))
FINE_AXES = ("x", "yl", "core", "z", "yh")
PLANE = ("yl", "x")
BF16 = jnp.bfloat16
F32 = jnp.float32
PLUS_FOUR = ((1, 4), (-1, 3))
MINUS_FOUR = ((-1, 4), (1, 3))


def dot32(left, right, dims=(((1,), (0,)), ((), ()))):
    return lax.dot_general(left, right, dims, preferred_element_type=F32)


def shifted(value, axis, step):
    size = lax.axis_size(axis)
    return lax.ppermute(value, axis, [(i, (i + step) % size) for i in range(size)])


def z_at(offset):
    return lax.rem(lax.axis_index("z") + offset + 8, 8)


def pick(blocks, index):
    return lax.dynamic_index_in_dim(blocks, index, 0, keepdims=False)


def put(whole, value, index):
    return lax.dynamic_update_index_in_dim(whole, value, index, 0)


def ordered(axis, mine, theirs):
    first = lax.axis_index(axis) == 0
    return jnp.concatenate(
        [jnp.where(first, mine, theirs), jnp.where(first, theirs, mine)], axis=0
    )


def gather_plane(block, name):
    with jax.named_scope(name + "_plane"):
        copies = jnp.broadcast_to(block[None], (8,) + block.shape)
        plane = lax.all_to_all(copies, PLANE, 0, 0, tiled=True)
        return plane.reshape((8 * block.shape[0], block.shape[1]))


def gather_core(plane, name):
    with jax.named_scope(name + "_core"):
        copies = jnp.broadcast_to(plane[None], (2,) + plane.shape)
        both = lax.all_to_all(copies, "core", 0, 0, tiled=True)
        return both.reshape((2 * plane.shape[0], plane.shape[1]))


def scatter(partials):
    core = lax.axis_index("core")
    halves = [p.reshape((2, p.shape[0] // 2, p.shape[1])) for p in partials]
    with jax.named_scope("outputs_core"):
        sent = jnp.concatenate([pick(h, 1 - core) for h in halves], axis=1)
        total = jnp.concatenate([pick(h, core) for h in halves], axis=1) + shifted(sent, "core", 1)
    with jax.named_scope("outputs_plane"):
        blocks = total.reshape((8, total.shape[0] // 8, total.shape[1]))
        came = lax.all_to_all(blocks, PLANE, 0, 0, tiled=True)
        total = jnp.sum(came.astype(F32), axis=0).astype(BF16)
        width = partials[0].shape[1]
        return total[:, :width], total[:, width:]


class SumRing:
    def __init__(self, name, terms, ways):
        self.name, self.ways = name, ways
        self.blocks = terms.reshape((8, terms.shape[0] // 8, terms.shape[1]))
        self.held = [pick(self.blocks, z_at(way * steps)) for way, steps in ways]

    def step(self, number):
        for ring, (way, steps) in enumerate(self.ways):
            left = steps - number
            if left < 0:
                continue
            with jax.named_scope(self.name):
                came = shifted(self.held[ring], "z", way)
                if left > 0:
                    source, came = lax.optimization_barrier((self.blocks, came))
                    came = came + pick(source, z_at(way * left))
                self.held[ring] = came

    def total(self, ahead=None):
        value = pick(self.blocks, z_at(0)).astype(F32)
        for came in self.held:
            value = value + came.astype(F32)
        yh = lax.axis_index("yh")
        halves = value.reshape((2, value.shape[0] // 2, value.shape[1]))
        with jax.named_scope(self.name + "_yh"):
            sent = pick(halves, 1 - yh).astype(BF16)
            if ahead is not None:
                sent = sent + ahead[:1, :1] * 0
            came = shifted(sent, "yh", 1)
            return pick(halves, yh) + came.astype(F32)


class CopyRing:
    def __init__(self, name, mine, ways):
        self.name, self.ways = name, ways
        with jax.named_scope(name + "_yh"):
            pair = ordered("yh", mine, shifted(mine, "yh", 1))
        self.held = [pair for _ in ways]
        self.whole = put(jnp.zeros((8,) + pair.shape, pair.dtype), pair, z_at(0))

    def step(self, number):
        for ring, (way, steps) in enumerate(self.ways):
            if number <= steps:
                with jax.named_scope(self.name):
                    self.held[ring] = shifted(self.held[ring], "z", way)
                self.whole = put(self.whole, self.held[ring], z_at(-way * number))

    def rows(self):
        return self.whole.reshape((-1, self.whole.shape[2]))


def run(rings, numbers=(1, 2, 3, 4)):
    for number in numbers:
        for ring in rings:
            ring.step(number)


def body(tokens, w_gate, w_up, w_down, grad_out):
    width = tokens.shape[1]
    plane = gather_plane(jnp.concatenate([tokens, grad_out], axis=1), "inputs")
    whole = gather_core(plane, "inputs")
    tokens, grads = whole[:, :width], whole[:, width:]
    gate = SumRing("gate", dot32(tokens, w_gate).astype(BF16), PLUS_FOUR)
    up = SumRing("up", dot32(tokens, w_up).astype(BF16), MINUS_FOUR)
    down = SumRing("down", dot32(grads, w_down, BACK_DIMS).astype(BF16), PLUS_FOUR)
    run((gate, up, down))
    gate_sum, up_sum = gate.total(), up.total()
    hidden_part = (gate_sum * jax.nn.sigmoid(gate_sum) * up_sum).astype(BF16)
    hidden = CopyRing("hidden", hidden_part, PLUS_FOUR)
    grad_hidden = down.total(hidden_part)
    gate_sum, up_sum = lax.optimization_barrier((gate_sum, up_sum))
    sigmoid_gate = jax.nn.sigmoid(gate_sum)
    grad_gate = CopyRing(
        "grad_gate",
        (
            grad_hidden * up_sum * sigmoid_gate * (1.0 + gate_sum * (1.0 - sigmoid_gate))
        ).astype(BF16),
        MINUS_FOUR,
    )
    grad_up = CopyRing("grad_up", (grad_hidden * (gate_sum * sigmoid_gate)).astype(BF16), PLUS_FOUR)
    run((hidden, grad_gate, grad_up))
    hidden, grad_gate, grad_up = hidden.rows(), grad_gate.rows(), grad_up.rows()
    mixed, grad_tokens = scatter(
        [
            dot32(hidden, w_down).astype(BF16),
            (dot32(grad_gate, w_gate, BACK_DIMS) + dot32(grad_up, w_up, BACK_DIMS)).astype(BF16),
        ]
    )
    grad_scale = 1.0 / math.sqrt(tokens.shape[0])
    with jax.named_scope("weight_grads"):
        grad_w_gate = (dot32(tokens, grad_gate, ROWS_DIMS) * grad_scale).astype(BF16)
        grad_w_up = (dot32(tokens, grad_up, ROWS_DIMS) * grad_scale).astype(BF16)
        grad_w_down = (dot32(hidden, grads, ROWS_DIMS) * grad_scale).astype(BF16)
    return (mixed, grad_tokens, grad_w_gate, grad_w_up, grad_w_down)


def solution(mesh):
    fine = Mesh(mesh.devices.reshape((4, 2, 2, 8, 2)), FINE_AXES)
    token_spec = P(("yl", "core", "x"), ("z", "yh"))
    in_specs = (
        token_spec,
        P(("z", "yh"), ("x", "yl", "core")),
        P(("z", "yh"), ("x", "yl", "core")),
        P(("x", "yl", "core"), ("z", "yh")),
        token_spec,
    )
    out_specs = (token_spec, token_spec) + in_specs[1:4]
    return jax.shard_map(body, mesh=fine, in_specs=in_specs, out_specs=out_specs, check_vma=False)
```

```python
import math

import jax
import jax.numpy as jnp
from jax import lax
from jax.sharding import Mesh, PartitionSpec as P

BACK_DIMS = (((1,), (1,)), ((), ()))
ROWS_DIMS = (((0,), (0,)), ((), ()))
FINE_AXES = ("x", "yl", "core", "z", "yh")
PLANE = ("yl", "x")
BF16 = jnp.bfloat16
F32 = jnp.float32
PLUS_FOUR = ((1, 4), (-1, 3))
MINUS_FOUR = ((-1, 4), (1, 3))


def dot32(left, right, dims=(((1,), (0,)), ((), ()))):
    return lax.dot_general(left, right, dims, preferred_element_type=F32)


def shifted(value, axis, step):
    size = lax.axis_size(axis)
    return lax.ppermute(value, axis, [(i, (i + step) % size) for i in range(size)])


def z_at(offset):
    return lax.rem(lax.axis_index("z") + offset + 8, 8)


def pick(blocks, index):
    return lax.dynamic_index_in_dim(blocks, index, 0, keepdims=False)


def put(whole, value, index):
    return lax.dynamic_update_index_in_dim(whole, value, index, 0)


def ordered(axis, mine, theirs):
    first = lax.axis_index(axis) == 0
    return jnp.concatenate(
        [jnp.where(first, mine, theirs), jnp.where(first, theirs, mine)], axis=0
    )


def gather_plane(block, name):
    with jax.named_scope(name + "_plane"):
        copies = jnp.broadcast_to(block[None], (8,) + block.shape)
        plane = lax.all_to_all(copies, PLANE, 0, 0, tiled=True)
        return plane.reshape((8 * block.shape[0], block.shape[1]))


def gather_core(plane, name):
    with jax.named_scope(name + "_core"):
        copies = jnp.broadcast_to(plane[None], (2,) + plane.shape)
        both = lax.all_to_all(copies, "core", 0, 0, tiled=True)
        return both.reshape((2 * plane.shape[0], plane.shape[1]))


def scatter(partials):
    core = lax.axis_index("core")
    halves = [p.reshape((2, p.shape[0] // 2, p.shape[1])) for p in partials]
    with jax.named_scope("outputs_core"):
        sent = jnp.concatenate([pick(h, 1 - core) for h in halves], axis=1)
        total = jnp.concatenate([pick(h, core) for h in halves], axis=1) + shifted(sent, "core", 1)
    with jax.named_scope("outputs_plane"):
        blocks = total.reshape((8, total.shape[0] // 8, total.shape[1]))
        came = lax.all_to_all(blocks, PLANE, 0, 0, tiled=True)
        total = jnp.sum(came.astype(F32), axis=0).astype(BF16)
        width = partials[0].shape[1]
        return total[:, :width], total[:, width:]


class SumRing:
    def __init__(self, name, terms, ways):
        self.name, self.ways = name, ways
        self.blocks = terms.reshape((8, terms.shape[0] // 8, terms.shape[1]))
        self.held = [pick(self.blocks, z_at(way * steps)) for way, steps in ways]

    def step(self, number):
        for ring, (way, steps) in enumerate(self.ways):
            left = steps - number
            if left < 0:
                continue
            with jax.named_scope(self.name):
                came = shifted(self.held[ring], "z", way)
                if left > 0:
                    source, came = lax.optimization_barrier((self.blocks, came))
                    came = came + pick(source, z_at(way * left))
                self.held[ring] = came

    def total(self, ahead=None):
        value = pick(self.blocks, z_at(0)).astype(F32)
        for came in self.held:
            value = value + came.astype(F32)
        yh = lax.axis_index("yh")
        halves = value.reshape((2, value.shape[0] // 2, value.shape[1]))
        with jax.named_scope(self.name + "_yh"):
            sent = pick(halves, 1 - yh).astype(BF16)
            if ahead is not None:
                sent = sent + ahead[:1, :1] * 0
            came = shifted(sent, "yh", 1)
            return pick(halves, yh) + came.astype(F32)


class CopyRing:
    def __init__(self, name, mine, ways):
        self.name, self.ways = name, ways
        with jax.named_scope(name + "_yh"):
            pair = ordered("yh", mine, shifted(mine, "yh", 1))
        self.held = [pair for _ in ways]
        self.whole = put(jnp.zeros((8,) + pair.shape, pair.dtype), pair, z_at(0))

    def step(self, number):
        for ring, (way, steps) in enumerate(self.ways):
            if number <= steps:
                with jax.named_scope(self.name):
                    self.held[ring] = shifted(self.held[ring], "z", way)
                self.whole = put(self.whole, self.held[ring], z_at(-way * number))

    def rows(self):
        return self.whole.reshape((-1, self.whole.shape[2]))


def run(rings, numbers=(1, 2, 3, 4)):
    for number in numbers:
        for ring in rings:
            ring.step(number)


def body(tokens, w_gate, w_up, w_down, grad_out):
    width = tokens.shape[1]
    plane = gather_plane(jnp.concatenate([tokens, grad_out], axis=1), "inputs")
    whole = gather_core(plane, "inputs")
    tokens, grads = whole[:, :width], whole[:, width:]
    gate = SumRing("gate", dot32(tokens, w_gate).astype(BF16), PLUS_FOUR)
    up = SumRing("up", dot32(tokens, w_up).astype(BF16), MINUS_FOUR)
    down = SumRing("down", dot32(grads, w_down, BACK_DIMS).astype(BF16), PLUS_FOUR)
    run((down, gate, up))
    gate_sum, up_sum = gate.total(), up.total()
    hidden_part = (gate_sum * jax.nn.sigmoid(gate_sum) * up_sum).astype(BF16)
    hidden = CopyRing("hidden", hidden_part, MINUS_FOUR)
    grad_hidden = down.total(hidden_part)
    gate_sum, up_sum = lax.optimization_barrier((gate_sum, up_sum))
    sigmoid_gate = jax.nn.sigmoid(gate_sum)
    grad_gate = CopyRing(
        "grad_gate",
        (
            grad_hidden * up_sum * sigmoid_gate * (1.0 + gate_sum * (1.0 - sigmoid_gate))
        ).astype(BF16),
        PLUS_FOUR,
    )
    grad_up = CopyRing("grad_up", (grad_hidden * (gate_sum * sigmoid_gate)).astype(BF16), MINUS_FOUR)
    run((hidden, grad_gate, grad_up))
    hidden, grad_gate, grad_up = hidden.rows(), grad_gate.rows(), grad_up.rows()
    mixed, grad_tokens = scatter(
        [
            dot32(hidden, w_down).astype(BF16),
            (dot32(grad_gate, w_gate, BACK_DIMS) + dot32(grad_up, w_up, BACK_DIMS)).astype(BF16),
        ]
    )
    grad_scale = 1.0 / math.sqrt(tokens.shape[0])
    with jax.named_scope("weight_grads"):
        grad_w_gate = (dot32(tokens, grad_gate, ROWS_DIMS) * grad_scale).astype(BF16)
        grad_w_up = (dot32(tokens, grad_up, ROWS_DIMS) * grad_scale).astype(BF16)
        grad_w_down = (dot32(hidden, grads, ROWS_DIMS) * grad_scale).astype(BF16)
    return (mixed, grad_tokens, grad_w_gate, grad_w_up, grad_w_down)


def solution(mesh):
    fine = Mesh(mesh.devices.reshape((4, 2, 2, 8, 2)), FINE_AXES)
    token_spec = P(("yl", "core", "x"), ("z", "yh"))
    in_specs = (
        token_spec,
        P(("z", "yh"), ("x", "yl", "core")),
        P(("z", "yh"), ("x", "yl", "core")),
        P(("x", "yl", "core"), ("z", "yh")),
        token_spec,
    )
    out_specs = (token_spec, token_spec) + in_specs[1:4]
    return jax.shard_map(body, mesh=fine, in_specs=in_specs, out_specs=out_specs, check_vma=False)
```
